32 devices in a mesh: groups: 2 (over x), section: 8 (over z, y), tensor: 2 (over core).
Axes of the slice: x: 2, y: 2, z: 4, core: 2. Of those that a mesh axis runs over, the one named last changes fastest.
Arguments:
- prompt_states: bfloat16 [16384, 8192], P(('groups', 'section')), parts along dimension 0, may hold values from -6 to 6
- norm_gain: bfloat16 [8192], replicated, may hold values from 0.5 to 1.5
- w_kv: bfloat16 [8192, 2, 512], P(None, None, 'tensor'), may hold values from -0.0625 to 0.0625
- pool_cache: bfloat16 [768, 64, 2, 512], P(('groups', 'section'), None, None, 'tensor'), parts along dimension 0, may hold values from -6 to 6
- queries: bfloat16 [64, 4, 4096], P(('groups', 'section'), None, 'tensor'), parts along dimension 0, may hold values from -110 to 110
- new_kv: bfloat16 [64, 4, 2, 512], P(('groups', 'section'), None, None, 'tensor'), parts along dimension 0, may hold values from -6 to 6
- ship_dest: int32 [256, 1], P('groups'), parts along dimension 0, may hold values from 0 to 7, as said below
- page_row: int32 [256], P('groups'), parts along dimension 0, may hold values from 0 to 3, as said below
- finished: int32 [256], P('groups'), parts along dimension 0, may hold values from 0 to 1, as said below
- page_table: int32 [64, 12], P('groups'), parts along dimension 0, may hold values from 0 to 383, as said below
- row_length: int32 [64], P('groups'), parts along dimension 0, may hold values from 1 to 768, as said below
Outputs:
- attended: bfloat16 [64, 4, 4096], P(('groups', 'section'), None, 'tensor'), parts along dimension 0
The draws below stay inside these ranges and needn't reach their ends.
There are 2 independent parts, one for each index of `groups`. The reference program is written for one: setup_inputs(seed, part) draws one part's arguments, and reference() takes and returns one part's arrays. A program takes and returns all parts, laid end to end along the dimension named above; an argument that names none is the same for every part. Nothing has to cross between parts.
Inputs may be any that keep to these rules, and one draw needn't show every extreme that they name: `page_table`: distinct resident page ids; the largest is reached. `row_length`: the longest row fills all 12 pages. `ship_dest`: the prompt pages of one device form whole prompts, each a run of consecutive pages with one owner, one row and one finished flag; a device hands at most one prompt of at most 3 pages to one owner, and on every device some owner gets exactly 3. `page_row`: equal over the pages of one prompt. `finished`: equal over the pages of one prompt.
All inputs are finite; a program needn't handle non-finite values.
Results may differ from the reference program's by a relative error of at most 0.012.
The reference program's roundings to bfloat16 on the way count: a program that leaves them out, or rounds other values in their place, can miss the bound.
Values may be sent and summed in bfloat16 or wider, within the bound.
A program may use at most 128 MiB of HBM per device.

```python
import math
import jax
import jax.numpy as jnp
from jax import lax

D = 8192
HS = 128
KVH = 4
QPK = 8
PAGE = 64
STEPS = 4
MAXP = 12
CAP = 3
PPD = 16
POOL = 48
ROWS_DEV = 4
PTOK_DEV = 1024
ROWS = 32
N_SECTION = 8


def prompt_plan(key):
    key = jax.random.fold_in(key, 29)
    order_key, score_key, hot_key, row_key, done_key = jax.random.split(key, 5)
    slot_count = N_SECTION * CAP
    block_keys = jax.random.split(order_key, N_SECTION)
    orders = jax.vmap(lambda one_key: jax.random.permutation(one_key, N_SECTION))(block_keys).astype(jnp.int32)
    favour = jax.random.randint(hot_key, (N_SECTION,), 0, 4)
    raw_scores = jax.random.randint(score_key, (N_SECTION, N_SECTION, CAP), 0, 1000)
    bias = favour[orders] * 300
    position_ids = jnp.arange(N_SECTION, dtype=jnp.int32)
    scores = jnp.where(position_ids[None, :, None] == 0, 5000, raw_scores + bias[:, :, None])
    distinct = scores.reshape(N_SECTION, slot_count) * slot_count + jnp.arange(slot_count, dtype=jnp.int32)[None, :]
    _, picked = lax.top_k(distinct, PPD)
    chosen = jnp.sum((picked[:, :, None] == jnp.arange(slot_count, dtype=jnp.int32)[None, None, :]).astype(jnp.int32), axis=1)
    counts = jnp.sum(chosen.reshape(N_SECTION, N_SECTION, CAP), axis=-1)
    ends = jnp.cumsum(counts, axis=1)
    page_ids = jnp.arange(PPD, dtype=jnp.int32)
    position_of = jnp.sum((page_ids[None, :, None] >= ends[:, None, :]).astype(jnp.int32), axis=-1)
    owners = jnp.take_along_axis(orders, position_of, axis=1)
    rows = jax.random.randint(row_key, (N_SECTION, N_SECTION), 0, ROWS_DEV)
    rows = rows.at[0, 0].set(ROWS_DEV - 1)
    done = (jax.random.randint(done_key, (N_SECTION, N_SECTION), 0, 4) < 3).astype(jnp.int32)
    done = done.at[0, 0].set(1).at[1, 0].set(0)
    row_of = jnp.take_along_axis(rows, position_of, axis=1)
    done_of = jnp.take_along_axis(done, position_of, axis=1)
    return (owners.reshape(-1).astype(jnp.int32), row_of.reshape(-1).astype(jnp.int32), done_of.reshape(-1).astype(jnp.int32))


def draw_ship_dest(key, part):
    owners, rows, done = prompt_plan(key)
    return owners.reshape(N_SECTION * PPD, 1)


def draw_page_row(key, part):
    owners, rows, done = prompt_plan(key)
    return rows


def draw_finished(key, part):
    owners, rows, done = prompt_plan(key)
    return done


def draw_page_table(key, part):
    key = jax.random.fold_in(key, 11)
    order = jax.random.permutation(key, N_SECTION * POOL)[:ROWS * MAXP]
    order = order + (N_SECTION * POOL - 1 - jnp.max(order))
    return order.reshape(ROWS, MAXP).astype(jnp.int32)


def draw_row_length(key, part):
    key = jax.random.fold_in(key, 12)
    first_key, second_key, pick_key = jax.random.split(key, 3)
    longest = MAXP * PAGE
    first_draw = jax.random.randint(first_key, (ROWS,), 1, longest + 1)
    second_draw = jax.random.randint(second_key, (ROWS,), 1, longest + 1)
    lengths = jnp.minimum(first_draw, second_draw)
    chosen = jax.random.randint(pick_key, (), 0, ROWS)
    return jnp.where(jnp.arange(ROWS) == chosen, longest, lengths).astype(jnp.int32)


def draw_queries(key, part):
    key = jax.random.fold_in(key, 13)
    dims = (ROWS, STEPS, KVH * QPK * HS)
    base_key = jax.random.fold_in(key, 0)
    values = jnp.clip(jax.random.normal(base_key, dims, jnp.float32), -6.0, 6.0)
    return values.astype(jnp.bfloat16)


def level_of(key, shape, pieces, smallest, top_value):
    level = 1.0
    for position, blocks in pieces:
        heights = jax.random.uniform(jax.random.fold_in(jax.random.fold_in(key, 6), position), (blocks,), jnp.float32, smallest / len(pieces), top_value / len(pieces))
        level = level * jnp.repeat(jnp.exp(heights), shape[position] // blocks).reshape((-1,) + (1,) * (len(shape) - 1 - position))
    return level


def centred(rng, extent, scale, most, cuts=(), held_as=jnp.bfloat16):
    factor_of = level_of(rng, extent, cuts, -0.22, 0.18) if cuts else 1.0
    values = jax.random.normal(rng, extent, jnp.float32) * scale * factor_of
    return jnp.minimum(jnp.maximum(values, -most), most).astype(held_as)


def setup_inputs(seed: int = 0, part: int = 0) -> dict:
    streams_of = jax.random.split(jax.random.key(seed), 12)
    own_keys = jax.random.split(jax.random.fold_in(streams_of[11], part), 12)
    return {
        "prompt_states": centred(own_keys[0], (N_SECTION * PTOK_DEV, D), 1.0, 6.0, ((0, 8),)),
        "norm_gain": jnp.clip(1.0 + 0.1 * jax.random.normal(streams_of[1], (D,), jnp.float32), 0.5, 1.5).astype(jnp.bfloat16),
        "w_kv": centred(streams_of[2], (D, 2, KVH * HS), D ** -0.5, 0.0625, ((2, 2),)),
        "pool_cache": centred(own_keys[3], (N_SECTION * POOL, PAGE, 2, KVH * HS), 1.0, 6.0, ((0, 8), (3, 2))),
        "queries": draw_queries(jax.random.fold_in(jax.random.fold_in(streams_of[11], part), 71), part),
        "new_kv": centred(own_keys[5], (ROWS, STEPS, 2, KVH * HS), 1.0, 6.0, ((0, 8), (3, 2))),
        "ship_dest": draw_ship_dest(jax.random.fold_in(jax.random.fold_in(streams_of[11], part), 71), part),
        "page_row": draw_page_row(jax.random.fold_in(jax.random.fold_in(streams_of[11], part), 71), part),
        "finished": draw_finished(jax.random.fold_in(jax.random.fold_in(streams_of[11], part), 71), part),
        "page_table": draw_page_table(jax.random.fold_in(jax.random.fold_in(streams_of[11], part), 71), part),
        "row_length": draw_row_length(jax.random.fold_in(jax.random.fold_in(streams_of[11], part), 71), part),
    }


masked_value = -1e+30
norm_epsilon = 1e-05

def reference(prompt_states, norm_gain, w_kv, pool_cache, queries, new_kv, ship_dest, page_row, finished, page_table, row_length):
    score_scale = 1.0 / math.sqrt(HS)
    states = prompt_states.astype(jnp.float32)
    spread = lax.rsqrt(lax.optimization_barrier(jnp.mean(states * states, axis=-1, keepdims=True)) + norm_epsilon)
    normed = (states * spread * norm_gain.astype(jnp.float32)).astype(jnp.bfloat16)
    prompt_keys = jnp.dot(normed, w_kv[:, 0], preferred_element_type=jnp.float32).astype(jnp.bfloat16)
    prompt_values = jnp.dot(normed, w_kv[:, 1], preferred_element_type=jnp.float32).astype(jnp.bfloat16)
    prompt_rows = jnp.repeat((ship_dest[:, 0] * ROWS_DEV + page_row).astype(jnp.int32), PAGE)
    prompt_live = jnp.repeat(finished == 1, PAGE)
    positions = jnp.arange(MAXP * PAGE, dtype=jnp.int32)
    step_ids = jnp.arange(STEPS, dtype=jnp.int32)
    causal = step_ids[:, None] >= step_ids[None, :]

    def one_row(row_index):
        chosen = pool_cache[page_table[row_index]].reshape(MAXP * PAGE, 2, KVH * HS)
        keys = jnp.concatenate([chosen[:, 0], prompt_keys, new_kv[row_index, :, 0]], axis=0)
        values = jnp.concatenate([chosen[:, 1], prompt_values, new_kv[row_index, :, 1]], axis=0)
        keys = keys.astype(jnp.float32).reshape(-1, KVH, HS)
        values = values.astype(jnp.float32).reshape(-1, KVH, HS)
        token_valid = jnp.concatenate([positions < row_length[row_index], prompt_live & (prompt_rows == row_index)])
        valid = jnp.concatenate([jnp.broadcast_to(token_valid[None, :], (STEPS, token_valid.shape[0])), causal], axis=1)
        grouped = queries[row_index].astype(jnp.float32).reshape(STEPS, KVH, QPK, HS)
        scores = jnp.einsum('sgqe,kge->sgqk', grouped, keys, precision=lax.Precision.HIGHEST) * score_scale
        scores = jnp.where(valid[:, None, None, :], scores, masked_value)
        tops = lax.optimization_barrier(jnp.max(scores, axis=-1, keepdims=True))
        weights = jnp.exp(scores - tops)
        totals = lax.optimization_barrier(jnp.sum(weights, axis=-1))
        rounded = lax.optimization_barrier(weights.astype(jnp.bfloat16)).astype(jnp.float32)
        summed = jnp.einsum('sgqk,kge->sgqe', rounded, values, precision=lax.Precision.HIGHEST)
        return (summed / totals[..., None]).reshape(STEPS, KVH * QPK * HS).astype(jnp.bfloat16)
    return lax.map(one_row, jnp.arange(ROWS, dtype=jnp.int32))
```

```python
import functools
import math

import jax
import jax.numpy as jnp
from jax import lax
from jax.experimental import pallas as pl
from jax.experimental.pallas import tpu as pltpu
from jax.sharding import PartitionSpec as P

HS = 128
MESH = pl.DeviceIdType.MESH
masked_value = -1e30
norm_epsilon = 1e-05
VMEM_LIMIT = 48 * 1024 * 1024
UNROLL = 4


def vmem():
    return pl.BlockSpec(memory_space=pltpu.VMEM)


def smem():
    return pl.BlockSpec(memory_space=pltpu.SMEM)


def greet(n, me):
    barrier = pltpu.get_barrier_semaphore()
    for k in range(1, n):
        pl.semaphore_signal(
            barrier, inc=1, device_id={"section": lax.rem(me + k, n)}, device_id_type=MESH
        )
    pl.semaphore_wait(barrier, n - 1)


def gather_kernel(n, own_ref, all_ref, send_sem, recv_sem):
    me = lax.axis_index("section")
    greet(n, me)
    copies = []
    for k in range(1, n):
        copy = pltpu.make_async_remote_copy(
            src_ref=own_ref,
            dst_ref=all_ref.at[me],
            send_sem=send_sem.at[k],
            recv_sem=recv_sem.at[k],
            device_id={"section": lax.rem(me + k, n)},
            device_id_type=MESH,
        )
        copy.start()
        copies.append(copy)
    all_ref[me] = own_ref[...]
    for copy in copies:
        copy.wait()


def attend_kernel(
    rows_dev, n, rows_ref, counts_ref, q_ref, pool_k, pool_v, prompt_k, prompt_v, fresh_k, fresh_v,
    out_ref, ml_ref, acc, tops, totals,
):
    span = q_ref.shape[0] // (n * rows_dev)
    half = span // 2
    page_len = 64
    pool_pages = pool_k.shape[0] // page_len
    prompt_pages = prompt_k.shape[0] // page_len
    scale = 1.0 / math.sqrt(HS)
    acc[...] = jnp.zeros_like(acc)
    totals[...] = jnp.zeros_like(totals)
    tops[...] = jnp.full_like(tops, masked_value)
    token = lax.broadcasted_iota(jnp.int32, (span, page_len), 1)
    line = lax.broadcasted_iota(jnp.int32, (span, page_len), 0)
    step = lax.rem(line, half) // 8
    contract_last = (((1,), (1,)), ((), ()))

    def page_part(row, count, keys, values, at, causal):
        q = q_ref[pl.ds(pl.multiple_of(row * span, span), span), :]
        k = keys[pl.ds(pl.multiple_of(at * page_len, page_len), page_len), :]
        v = values[pl.ds(pl.multiple_of(at * page_len, page_len), page_len), :]
        low = lax.dot_general(
            q[:half], k[:, :HS], contract_last, preferred_element_type=jnp.float32
        )
        high = lax.dot_general(
            q[half:], k[:, HS:], contract_last, preferred_element_type=jnp.float32
        )
        scores = jnp.concatenate([low, high], axis=0) * scale
        usable = (token <= step) if causal else (token < count)
        scores = jnp.where(usable, scores, masked_value)
        top = jnp.max(scores, axis=1, keepdims=True)
        weights = jnp.where(usable, jnp.exp(scores - top), 0.0)
        total = jnp.sum(weights, axis=1, keepdims=True)
        main = weights.astype(jnp.bfloat16)
        rest = (weights - main.astype(jnp.float32)).astype(jnp.bfloat16)
        both_low = jnp.concatenate([main[:half], rest[:half]], axis=0)
        both_high = jnp.concatenate([main[half:], rest[half:]], axis=0)
        sum_low = jnp.dot(both_low, v[:, :HS], preferred_element_type=jnp.float32)
        sum_high = jnp.dot(both_high, v[:, HS:], preferred_element_type=jnp.float32)
        summed = jnp.concatenate(
            [sum_low[:half] + sum_low[half:], sum_high[:half] + sum_high[half:]], axis=0
        )
        return top, total, summed

    def update(row, part):
        top, total, summed = part
        place = pl.ds(pl.multiple_of(row * span, span), span)
        old = tops[place, :]
        new = jnp.maximum(old, top)
        keep = jnp.exp(old - new)
        add = jnp.exp(top - new)
        tops[place, :] = new
        totals[place, :] = totals[place, :] * keep + total * add
        acc[place, :] = acc[place, :] * keep + summed * add

    def run(first, pages, keys, values, causal):
        def some(i, _):
            parts = []
            for u in range(UNROLL):
                at = i * UNROLL + u
                row = rows_ref[first + at]
                parts.append((row, page_part(row, counts_ref[first + at], keys, values, at, causal)))
            for row, part in parts:
                update(row, part)
            return 0

        lax.fori_loop(0, pages // UNROLL, some, 0)

    run(0, pool_pages, pool_k, pool_v, False)
    run(pool_pages, prompt_pages, prompt_k, prompt_v, False)
    run(pool_pages + prompt_pages, rows_dev, fresh_k, fresh_v, True)

    block = rows_dev * span
    lane = lax.broadcasted_iota(jnp.int32, (block, HS), 1)
    for d in range(n):
        here = pl.ds(d * block, block)
        out_ref[d] = acc[here, :].astype(jnp.bfloat16)
        mixed = jnp.where(lane == 0, tops[here, :], totals[here, :])
        ml_ref[d] = mixed.T[:8, :]


def merge_kernel(n, part_ref, ml_ref, out_ref, parts, mls, coef, send_sem, recv_sem):
    me = lax.axis_index("section")
    greet(n, me)
    copies = []
    for k in range(1, n):
        to = lax.rem(me + k, n)
        for which, (src, dst) in enumerate(((part_ref, parts), (ml_ref, mls))):
            copy = pltpu.make_async_remote_copy(
                src_ref=src.at[to],
                dst_ref=dst.at[me],
                send_sem=send_sem.at[which, k],
                recv_sem=recv_sem.at[which, k],
                device_id={"section": to},
                device_id_type=MESH,
            )
            copy.start()
            copies.append(copy)
    parts[me] = part_ref[me]
    mls[me] = ml_ref[me]
    for copy in copies:
        copy.wait()
    top = mls[0, 0:1, :]
    for i in range(1, n):
        top = jnp.maximum(top, mls[i, 0:1, :])
    total = jnp.zeros_like(top)
    for i in range(n):
        total = total + jnp.exp(mls[i, 0:1, :] - top) * mls[i, 1:2, :]
    coef[...] = jnp.zeros_like(coef)
    for i in range(n):
        coef[i : i + 1, :] = jnp.exp(mls[i, 0:1, :] - top) / total
    columns = coef[...].T
    result = jnp.zeros(out_ref.shape, jnp.float32)
    for i in range(n):
        result = result + parts[i].astype(jnp.float32) * columns[:, i : i + 1]
    out_ref[...] = result.astype(jnp.bfloat16)


def body(
    prompt_states,
    norm_gain,
    w_kv,
    pool_cache,
    queries,
    new_kv,
    ship_dest,
    page_row,
    finished,
    page_table,
    row_length,
):
    n = lax.axis_size("section")
    me = lax.axis_index("section")
    rows_dev, steps, width_q = queries.shape
    pool_pages, page_len, _, width_kv = pool_cache.shape
    kv_heads = width_kv // HS
    group = width_q // width_kv
    prompt_pages = prompt_states.shape[0] // page_len
    all_rows, max_pages = page_table.shape
    span = kv_heads * steps * group
    block = rows_dev * span

    own_q = queries.reshape(rows_dev, steps, kv_heads, group, HS).transpose(0, 2, 1, 3, 4)
    own_q = own_q.reshape(block, HS)
    all_q = pl.pallas_call(
        functools.partial(gather_kernel, n),
        out_shape=jax.ShapeDtypeStruct((n, block, HS), jnp.bfloat16),
        in_specs=[vmem()],
        out_specs=vmem(),
        scratch_shapes=[pltpu.SemaphoreType.DMA((n,)), pltpu.SemaphoreType.DMA((n,))],
        compiler_params=pltpu.CompilerParams(
            collective_id=0, has_side_effects=True, vmem_limit_bytes=VMEM_LIMIT
        ),
    )(own_q)

    states = prompt_states.astype(jnp.float32)
    spread = lax.rsqrt(jnp.mean(states * states, axis=-1, keepdims=True) + norm_epsilon)
    normed = (states * spread * norm_gain.astype(jnp.float32)).astype(jnp.bfloat16)
    prompt_kv = jnp.einsum("td,dkc->ktc", normed, w_kv, preferred_element_type=jnp.float32).astype(
        jnp.bfloat16
    )

    page_ids = me * pool_pages + jnp.arange(pool_pages, dtype=jnp.int32)
    page_hits = page_table[:, :, None] == page_ids[None, None, :]
    token_fill = jnp.clip(
        row_length[:, None] - jnp.arange(max_pages, dtype=jnp.int32)[None, :] * page_len,
        0,
        page_len,
    )
    row_ids = jnp.arange(all_rows, dtype=jnp.int32)
    packed = token_fill * all_rows + row_ids[:, None]
    found = jnp.sum(jnp.where(page_hits, packed[:, :, None], 0), axis=(0, 1))
    own_pages = me * prompt_pages
    dest = lax.dynamic_slice_in_dim(ship_dest[:, 0], own_pages, prompt_pages, 0)
    joined = lax.dynamic_slice_in_dim(page_row, own_pages, prompt_pages, 0)
    done = lax.dynamic_slice_in_dim(finished, own_pages, prompt_pages, 0)
    own_rows = me * rows_dev + jnp.arange(rows_dev, dtype=jnp.int32)
    rows = jnp.concatenate([found % all_rows, dest * rows_dev + joined, own_rows])
    counts = jnp.concatenate(
        [
            found // all_rows,
            jnp.where(done == 1, page_len, 0).astype(jnp.int32),
            jnp.zeros((rows_dev,), jnp.int32),
        ]
    )
    pool_k = pool_cache[:, :, 0].reshape(pool_pages * page_len, width_kv)
    pool_v = pool_cache[:, :, 1].reshape(pool_pages * page_len, width_kv)
    fresh = jnp.pad(new_kv, ((0, 0), (0, page_len - steps), (0, 0), (0, 0)))
    fresh_k = fresh[:, :, 0].reshape(rows_dev * page_len, width_kv)
    fresh_v = fresh[:, :, 1].reshape(rows_dev * page_len, width_kv)

    parts, mls = pl.pallas_call(
        functools.partial(attend_kernel, rows_dev, n),
        out_shape=(
            jax.ShapeDtypeStruct((n, block, HS), jnp.bfloat16),
            jax.ShapeDtypeStruct((n, 8, block), jnp.float32),
        ),
        in_specs=[smem(), smem()] + [vmem()] * 7,
        out_specs=(vmem(), vmem()),
        scratch_shapes=[pltpu.VMEM((n * block, HS), jnp.float32)] * 3,
        compiler_params=pltpu.CompilerParams(vmem_limit_bytes=VMEM_LIMIT),
    )(
        rows, counts, all_q.reshape(n * block, HS), pool_k, pool_v, prompt_kv[0], prompt_kv[1],
        fresh_k, fresh_v,
    )

    merged = pl.pallas_call(
        functools.partial(merge_kernel, n),
        out_shape=jax.ShapeDtypeStruct((block, HS), jnp.bfloat16),
        in_specs=[vmem(), vmem()],
        out_specs=vmem(),
        scratch_shapes=[
            pltpu.VMEM((n, block, HS), jnp.bfloat16),
            pltpu.VMEM((n, 8, block), jnp.float32),
            pltpu.VMEM((HS, block), jnp.float32),
            pltpu.SemaphoreType.DMA((2, n)),
            pltpu.SemaphoreType.DMA((2, n)),
        ],
        compiler_params=pltpu.CompilerParams(
            collective_id=1, has_side_effects=True, vmem_limit_bytes=VMEM_LIMIT
        ),
    )(parts, mls)
    heads = merged.reshape(rows_dev, kv_heads, steps, group, HS).transpose(0, 2, 1, 3, 4)
    return heads.reshape(rows_dev, steps, width_q)


def solution(mesh):
    return jax.shard_map(
        body,
        mesh=mesh,
        in_specs=(
            P(("groups", "section"), None),
            P(),
            P(None, None, "tensor"),
            P(("groups", "section"), None, None, "tensor"),
            P(("groups", "section"), None, "tensor"),
            P(("groups", "section"), None, None, "tensor"),
            P("groups", None),
            P("groups"),
            P("groups"),
            P("groups", None),
            P("groups"),
        ),
        out_specs=P(("groups", "section"), None, "tensor"),
        check_vma=False,
    )
```

```python
import functools
import math

import jax
import jax.numpy as jnp
from jax import lax
from jax.experimental import pallas as pl
from jax.experimental.pallas import tpu as pltpu
from jax.sharding import PartitionSpec as P

HS = 128
MESH = pl.DeviceIdType.MESH
masked_value = -1e30
norm_epsilon = 1e-05
VMEM_LIMIT = 48 * 1024 * 1024
UNROLL = 4


def vmem():
    return pl.BlockSpec(memory_space=pltpu.VMEM)


def smem():
    return pl.BlockSpec(memory_space=pltpu.SMEM)


def greet(n, me):
    barrier = pltpu.get_barrier_semaphore()
    for k in range(1, n):
        pl.semaphore_signal(
            barrier, inc=1, device_id={"section": lax.rem(me + k, n)}, device_id_type=MESH
        )
    pl.semaphore_wait(barrier, n - 1)


def attend_kernel(
    rows_dev, n, rows_ref, counts_ref, lookup_ref, pool, prompt_k, prompt_v, fresh, *rest
):
    blocks = rest[:n]
    out_ref, ml_ref, q_ref, acc, tops, totals = rest[n:]
    for k in range(n):
        size = blocks[k].shape[0]
        q_ref[k * size : (k + 1) * size, :] = blocks[k][...]
    span = q_ref.shape[0] // (n * rows_dev)
    half = span // 2
    page_len = 64
    wide = 2 * page_len
    pool_pages = pool.shape[0] // wide
    prompt_pages = prompt_k.shape[0] // page_len
    scale = 1.0 / math.sqrt(HS)
    acc[...] = jnp.zeros_like(acc)
    totals[...] = jnp.zeros_like(totals)
    tops[...] = jnp.full_like(tops, masked_value)
    lane = lax.broadcasted_iota(jnp.int32, (span, wide), 1)
    line = lax.broadcasted_iota(jnp.int32, (span, wide), 0)
    step = lax.rem(line, half) // 8
    twice = jnp.where(lax.rem(lane, 2) == 0, lane // 2, page_len)
    contract_last = (((1,), (1,)), ((), ()))

    def load_pair(ref, at):
        return ref[pl.ds(pl.multiple_of(at * wide, wide), wide), :]

    def load_split(refs, at):
        here = pl.ds(pl.multiple_of(at * page_len, page_len), page_len)
        return jnp.concatenate([refs[0][here, :], refs[1][here, :]], axis=0)

    def page_part(place, count, pages, at, kind):
        q = q_ref[pl.ds(pl.multiple_of(place * span, span), span), :]
        kv = load_split(pages, at) if kind == "split" else load_pair(pages, at)
        low = lax.dot_general(
            q[:half], kv[:, :HS], contract_last, preferred_element_type=jnp.float32
        )
        high = lax.dot_general(
            q[half:], kv[:, HS:], contract_last, preferred_element_type=jnp.float32
        )
        scores = jnp.concatenate([low, high], axis=0) * scale
        if kind == "split":
            usable = lane < count
        elif kind == "fresh":
            usable = twice <= step
        else:
            usable = twice < count
        scores = jnp.where(usable, scores, masked_value)
        top = jnp.max(scores, axis=1, keepdims=True)
        weights = jnp.where(usable, jnp.exp(scores - top), 0.0)
        total = jnp.sum(weights, axis=1, keepdims=True)
        weights = pltpu.roll(weights, page_len if kind == "split" else 1, 1)
        main = weights.astype(jnp.bfloat16)
        rest = (weights - main.astype(jnp.float32)).astype(jnp.bfloat16)
        both_low = jnp.concatenate([main[:half], rest[:half]], axis=0)
        both_high = jnp.concatenate([main[half:], rest[half:]], axis=0)
        sum_low = jnp.dot(both_low, kv[:, :HS], preferred_element_type=jnp.float32)
        sum_high = jnp.dot(both_high, kv[:, HS:], preferred_element_type=jnp.float32)
        summed = jnp.concatenate(
            [sum_low[:half] + sum_low[half:], sum_high[:half] + sum_high[half:]], axis=0
        )
        return top, total, summed

    def update(row, part):
        top, total, summed = part
        place = pl.ds(pl.multiple_of(row * span, span), span)
        old = tops[place, :]
        new = jnp.maximum(old, top)
        keep = jnp.exp(old - new)
        add = jnp.exp(top - new)
        tops[place, :] = new
        totals[place, :] = totals[place, :] * keep + total * add
        acc[place, :] = acc[place, :] * keep + summed * add

    def run(first, count, pages, kind):
        def some(i, _):
            parts = []
            for u in range(UNROLL):
                at = i * UNROLL + u
                row = rows_ref[first + at]
                place = lookup_ref[first + at]
                parts.append((row, page_part(place, counts_ref[first + at], pages, at, kind)))
            for row, part in parts:
                update(row, part)
            return 0

        lax.fori_loop(0, count // UNROLL, some, 0)

    run(0, pool_pages, pool, "pair")
    run(pool_pages, prompt_pages, (prompt_k, prompt_v), "split")
    run(pool_pages + prompt_pages, rows_dev, fresh, "fresh")

    block = rows_dev * span
    lane = lax.broadcasted_iota(jnp.int32, (block, HS), 1)
    for d in range(n):
        here = pl.ds(d * block, block)
        out_ref[d] = acc[here, :].astype(jnp.bfloat16)
        mixed = jnp.where(lane == 0, tops[here, :], totals[here, :])
        ml_ref[d] = mixed.T[:8, :]


def merge_kernel(n, part_ref, ml_ref, out_ref, parts, mls, coef, send_sem, recv_sem):
    me = lax.axis_index("section")
    greet(n, me)
    copies = []
    for k in range(1, n):
        to = lax.rem(me + k, n)
        for which, (src, dst) in enumerate(((part_ref, parts), (ml_ref, mls))):
            copy = pltpu.make_async_remote_copy(
                src_ref=src.at[to],
                dst_ref=dst.at[me],
                send_sem=send_sem.at[which, k],
                recv_sem=recv_sem.at[which, k],
                device_id={"section": to},
                device_id_type=MESH,
            )
            copy.start()
            copies.append(copy)
    parts[me] = part_ref[me]
    mls[me] = ml_ref[me]
    for copy in copies:
        copy.wait()
    top = mls[0, 0:1, :]
    for i in range(1, n):
        top = jnp.maximum(top, mls[i, 0:1, :])
    total = jnp.zeros_like(top)
    for i in range(n):
        total = total + jnp.exp(mls[i, 0:1, :] - top) * mls[i, 1:2, :]
    coef[...] = jnp.zeros_like(coef)
    for i in range(n):
        coef[i : i + 1, :] = jnp.exp(mls[i, 0:1, :] - top) / total
    columns = coef[...].T
    result = jnp.zeros(out_ref.shape, jnp.float32)
    for i in range(n):
        result = result + parts[i].astype(jnp.float32) * columns[:, i : i + 1]
    out_ref[...] = result.astype(jnp.bfloat16)


def body(
    prompt_states,
    norm_gain,
    w_kv,
    pool_cache,
    queries,
    new_kv,
    ship_dest,
    page_row,
    finished,
    page_table,
    row_length,
):
    n = lax.axis_size("section")
    me = lax.axis_index("section")
    rows_dev, steps, width_q = queries.shape
    pool_pages, page_len, _, width_kv = pool_cache.shape
    kv_heads = width_kv // HS
    group = width_q // width_kv
    prompt_pages = prompt_states.shape[0] // page_len
    all_rows, max_pages = page_table.shape
    span = kv_heads * steps * group
    block = rows_dev * span

    own_q = queries.reshape(rows_dev, steps, kv_heads, group, HS).transpose(0, 2, 1, 3, 4)
    own_q = own_q.reshape(block, HS)
    blocks = [own_q] + [
        lax.ppermute(own_q, "section", [(i, (i + k) % n) for i in range(n)]) for k in range(1, n)
    ]

    states = prompt_states.astype(jnp.float32)
    spread = lax.rsqrt(jnp.mean(states * states, axis=-1, keepdims=True) + norm_epsilon)
    early = len(blocks) - 5
    if early > 1:
        spread, *first = lax.optimization_barrier((spread, *blocks[1:early]))
        blocks[1:early] = first
    normed = (states * spread * norm_gain.astype(jnp.float32)).astype(jnp.bfloat16)
    prompt_kv = jnp.einsum("td,dkc->ktc", normed, w_kv, preferred_element_type=jnp.float32).astype(
        jnp.bfloat16
    )

    page_ids = me * pool_pages + jnp.arange(pool_pages, dtype=jnp.int32)
    page_hits = page_table[:, :, None] == page_ids[None, None, :]
    token_fill = jnp.clip(
        row_length[:, None] - jnp.arange(max_pages, dtype=jnp.int32)[None, :] * page_len,
        0,
        page_len,
    )
    row_ids = jnp.arange(all_rows, dtype=jnp.int32)
    packed = token_fill * all_rows + row_ids[:, None]
    found = jnp.sum(jnp.where(page_hits, packed[:, :, None], 0), axis=(0, 1))
    own_pages = me * prompt_pages
    dest = lax.dynamic_slice_in_dim(ship_dest[:, 0], own_pages, prompt_pages, 0)
    joined = lax.dynamic_slice_in_dim(page_row, own_pages, prompt_pages, 0)
    done = lax.dynamic_slice_in_dim(finished, own_pages, prompt_pages, 0)
    own_rows = me * rows_dev + jnp.arange(rows_dev, dtype=jnp.int32)
    rows = jnp.concatenate([found % all_rows, dest * rows_dev + joined, own_rows])
    lookup = (me + n - rows // rows_dev) % n * rows_dev + rows % rows_dev
    counts = jnp.concatenate(
        [
            found // all_rows,
            jnp.where(done == 1, page_len, 0).astype(jnp.int32),
            jnp.zeros((rows_dev,), jnp.int32),
        ]
    )
    pool = pool_cache.reshape(pool_pages * page_len * 2, width_kv)
    fresh = jnp.pad(new_kv, ((0, 0), (0, page_len - steps), (0, 0), (0, 0)))
    fresh = fresh.reshape(rows_dev * page_len * 2, width_kv)

    parts, mls = pl.pallas_call(
        functools.partial(attend_kernel, rows_dev, n),
        out_shape=(
            jax.ShapeDtypeStruct((n, block, HS), jnp.bfloat16),
            jax.ShapeDtypeStruct((n, 8, block), jnp.float32),
        ),
        in_specs=[smem()] * 3 + [vmem()] * (4 + n),
        out_specs=(vmem(), vmem()),
        scratch_shapes=[pltpu.VMEM((n * block, HS), jnp.bfloat16)]
        + [pltpu.VMEM((n * block, HS), jnp.float32)] * 3,
        compiler_params=pltpu.CompilerParams(vmem_limit_bytes=VMEM_LIMIT),
    )(
        rows, counts, lookup, pool, prompt_kv[0], prompt_kv[1], fresh, *blocks,
    )

    merged = pl.pallas_call(
        functools.partial(merge_kernel, n),
        out_shape=jax.ShapeDtypeStruct((block, HS), jnp.bfloat16),
        in_specs=[vmem(), vmem()],
        out_specs=vmem(),
        scratch_shapes=[
            pltpu.VMEM((n, block, HS), jnp.bfloat16),
            pltpu.VMEM((n, 8, block), jnp.float32),
            pltpu.VMEM((HS, block), jnp.float32),
            pltpu.SemaphoreType.DMA((2, n)),
            pltpu.SemaphoreType.DMA((2, n)),
        ],
        compiler_params=pltpu.CompilerParams(
            collective_id=1, has_side_effects=True, vmem_limit_bytes=VMEM_LIMIT
        ),
    )(parts, mls)
    heads = merged.reshape(rows_dev, kv_heads, steps, group, HS).transpose(0, 2, 1, 3, 4)
    return heads.reshape(rows_dev, steps, width_q)


def solution(mesh):
    return jax.shard_map(
        body,
        mesh=mesh,
        in_specs=(
            P(("groups", "section"), None),
            P(),
            P(None, None, "tensor"),
            P(("groups", "section"), None, None, "tensor"),
            P(("groups", "section"), None, "tensor"),
            P(("groups", "section"), None, None, "tensor"),
            P("groups", None),
            P("groups"),
            P("groups"),
            P("groups", None),
            P("groups"),
        ),
        out_specs=P(("groups", "section"), None, "tensor"),
        check_vma=False,
    )
```

```python
import functools
import math

import jax
import jax.numpy as jnp
from jax import lax
from jax.experimental import pallas as pl
from jax.experimental.pallas import tpu as pltpu
from jax.sharding import PartitionSpec as P

HS = 128
MESH = pl.DeviceIdType.MESH
masked_value = -1e30
norm_epsilon = 1e-05
VMEM_LIMIT = 48 * 1024 * 1024
UNROLL = 8


def vmem():
    return pl.BlockSpec(memory_space=pltpu.VMEM)


def smem():
    return pl.BlockSpec(memory_space=pltpu.SMEM)


def greet(n, me):
    barrier = pltpu.get_barrier_semaphore()
    for k in range(1, n):
        pl.semaphore_signal(
            barrier, inc=1, device_id={"section": lax.rem(me + k, n)}, device_id_type=MESH
        )
    pl.semaphore_wait(barrier, n - 1)


def attend_kernel(
    rows_dev, n, pieces, rows_ref, counts_ref, lookup_ref, pool, prompt_k, prompt_v, fresh, *others
):
    blocks = others[:pieces]
    out_ref, ml_ref, q_ref, acc, tops, totals = others[pieces:]
    span = q_ref.shape[0] // (n * rows_dev)
    half = span // 2
    start = 0
    for piece in blocks:
        size = piece.shape[0]
        q = piece[...]
        of_low = lax.rem(lax.broadcasted_iota(jnp.int32, q.shape, 0), span) < half
        zero = jnp.zeros_like(q)
        q_ref[start : start + size, :HS] = jnp.where(of_low, q, zero)
        q_ref[start : start + size, HS:] = jnp.where(of_low, zero, q)
        start += size
    page_len = 64
    wide = 2 * page_len
    pool_pages = pool.shape[0] // wide
    prompt_pages = prompt_k.shape[0] // page_len
    scale = 1.0 / math.sqrt(HS)
    acc[...] = jnp.zeros_like(acc)
    totals[...] = jnp.zeros_like(totals)
    tops[...] = jnp.full_like(tops, masked_value)
    lane = lax.broadcasted_iota(jnp.int32, (span, wide), 1)
    line = lax.broadcasted_iota(jnp.int32, (span, wide), 0)
    step = lax.rem(line, half) // 8
    twice = jnp.where(lax.rem(lane, 2) == 0, lane // 2, page_len)
    contract_last = (((1,), (1,)), ((), ()))

    def load_pair(ref, at):
        return ref[pl.ds(pl.multiple_of(at * wide, wide), wide), :]

    def load_split(refs, at):
        here = pl.ds(pl.multiple_of(at * page_len, page_len), page_len)
        return jnp.concatenate([refs[0][here, :], refs[1][here, :]], axis=0)

    def page_part(place, count, pages, at, kind):
        q = q_ref[pl.ds(pl.multiple_of(place * span, span), span), :]
        kv = load_split(pages, at) if kind == "split" else load_pair(pages, at)
        scores = lax.dot_general(
            q, kv, contract_last, preferred_element_type=jnp.float32
        ) * scale
        if kind == "split":
            usable = lane < count
        elif kind == "fresh":
            usable = twice <= step
        else:
            usable = twice < count
        scores = jnp.where(usable, scores, masked_value)
        top = jnp.max(scores, axis=1, keepdims=True)
        weights = jnp.where(usable, jnp.exp(scores - top), 0.0)
        total = jnp.sum(weights, axis=1, keepdims=True)
        weights = pltpu.roll(weights, page_len if kind == "split" else 1, 1)
        main = weights.astype(jnp.bfloat16)
        rest = (weights - main.astype(jnp.float32)).astype(jnp.bfloat16)
        both_low = jnp.concatenate([main[:half], rest[:half]], axis=0)
        both_high = jnp.concatenate([main[half:], rest[half:]], axis=0)
        sum_low = jnp.dot(both_low, kv[:, :HS], preferred_element_type=jnp.float32)
        sum_high = jnp.dot(both_high, kv[:, HS:], preferred_element_type=jnp.float32)
        summed = jnp.concatenate(
            [sum_low[:half] + sum_low[half:], sum_high[:half] + sum_high[half:]], axis=0
        )
        return top, total, summed

    def update(row, part):
        top, total, summed = part
        place = pl.ds(pl.multiple_of(row * span, span), span)
        old = tops[place, :]
        new = jnp.maximum(old, top)
        keep = jnp.exp(old - new)
        add = jnp.exp(top - new)
        tops[place, :] = new
        totals[place, :] = totals[place, :] * keep + total * add
        acc[place, :] = acc[place, :] * keep + summed * add

    def run(first, count, pages, kind):
        many = math.gcd(count, UNROLL)

        def some(i, _):
            parts = []
            for u in range(many):
                at = i * many + u
                row = rows_ref[first + at]
                place = lookup_ref[first + at]
                parts.append((row, page_part(place, counts_ref[first + at], pages, at, kind)))
            for row, part in parts:
                update(row, part)
            return 0

        lax.fori_loop(0, count // many, some, 0)

    run(0, pool_pages, pool, "pair")
    run(pool_pages, prompt_pages, (prompt_k, prompt_v), "split")
    run(pool_pages + prompt_pages, rows_dev, fresh, "fresh")

    block = rows_dev * span
    lane = lax.broadcasted_iota(jnp.int32, (block, HS), 1)
    for d in range(n):
        here = pl.ds(d * block, block)
        out_ref[d] = acc[here, :].astype(jnp.bfloat16)
        mixed = jnp.where(lane == 0, tops[here, :], totals[here, :])
        ml_ref[d] = mixed.T[:8, :]


def merge_kernel(n, part_ref, ml_ref, out_ref, parts, mls, coef, send_sem, recv_sem):
    me = lax.axis_index("section")
    greet(n, me)
    copies = []
    for k in range(1, n):
        to = lax.rem(me + k, n)
        for which, (src, dst) in enumerate(((part_ref, parts), (ml_ref, mls))):
            copy = pltpu.make_async_remote_copy(
                src_ref=src.at[to],
                dst_ref=dst.at[me],
                send_sem=send_sem.at[which, k],
                recv_sem=recv_sem.at[which, k],
                device_id={"section": to},
                device_id_type=MESH,
            )
            copy.start()
            copies.append(copy)
    parts[me] = part_ref[me]
    mls[me] = ml_ref[me]
    for copy in copies:
        copy.wait()
    top = mls[0, 0:1, :]
    for i in range(1, n):
        top = jnp.maximum(top, mls[i, 0:1, :])
    total = jnp.zeros_like(top)
    for i in range(n):
        total = total + jnp.exp(mls[i, 0:1, :] - top) * mls[i, 1:2, :]
    coef[...] = jnp.zeros_like(coef)
    for i in range(n):
        coef[i : i + 1, :] = jnp.exp(mls[i, 0:1, :] - top) / total
    columns = coef[...].T
    result = jnp.zeros(out_ref.shape, jnp.float32)
    for i in range(n):
        result = result + parts[i].astype(jnp.float32) * columns[:, i : i + 1]
    out_ref[...] = result.astype(jnp.bfloat16)


def row_spread(prompts):
    states = prompts.astype(jnp.float32)
    return lax.rsqrt(jnp.mean(states * states, axis=-1, keepdims=True) + norm_epsilon)


def body(
    prompt_states,
    norm_gain,
    w_kv,
    pool_cache,
    queries,
    new_kv,
    ship_dest,
    page_row,
    finished,
    page_table,
    row_length,
):
    n = lax.axis_size("section")
    me = lax.axis_index("section")
    rows_dev, steps, width_q = queries.shape
    pool_pages, page_len, _, width_kv = pool_cache.shape
    kv_heads = width_kv // HS
    group = width_q // width_kv
    prompt_pages = prompt_states.shape[0] // page_len
    all_rows, max_pages = page_table.shape
    span = kv_heads * steps * group
    block = rows_dev * span

    own_q = queries.reshape(rows_dev, steps, kv_heads, group, HS).transpose(0, 2, 1, 3, 4)
    own_q = own_q.reshape(block, HS)
    blocks = [own_q]
    pool = pool_cache.reshape(pool_pages * page_len * 2, width_kv)
    prompts = prompt_states
    spread = None
    size = 1
    while size < n:
        whole = blocks[0] if size == 1 else jnp.concatenate(blocks, axis=0)
        other = lax.ppermute(whole, "section", [(i, i ^ size) for i in range(n)])
        if 2 * size == n:
            pass
        elif size == 1:
            other, pool, prompts = lax.optimization_barrier((other, pool, prompts))
        elif 4 * size == n:
            spread = row_spread(prompts)
            other, spread = lax.optimization_barrier((other, spread))
        blocks.append(other)
        size *= 2
    if spread is None:
        spread = row_spread(prompts)
    states = prompts.astype(jnp.float32)
    normed = (states * spread * norm_gain.astype(jnp.float32)).astype(jnp.bfloat16)
    prompt_kv = jnp.einsum("td,dkc->ktc", normed, w_kv, preferred_element_type=jnp.float32).astype(
        jnp.bfloat16
    )

    page_ids = me * pool_pages + jnp.arange(pool_pages, dtype=jnp.int32)
    page_hits = page_table[:, :, None] == page_ids[None, None, :]
    token_fill = jnp.clip(
        row_length[:, None] - jnp.arange(max_pages, dtype=jnp.int32)[None, :] * page_len,
        0,
        page_len,
    )
    row_ids = jnp.arange(all_rows, dtype=jnp.int32)
    packed = token_fill * all_rows + row_ids[:, None]
    found = jnp.sum(jnp.where(page_hits, packed[:, :, None], 0), axis=(0, 1))
    own_pages = me * prompt_pages
    dest = lax.dynamic_slice_in_dim(ship_dest[:, 0], own_pages, prompt_pages, 0)
    joined = lax.dynamic_slice_in_dim(page_row, own_pages, prompt_pages, 0)
    done = lax.dynamic_slice_in_dim(finished, own_pages, prompt_pages, 0)
    own_rows = me * rows_dev + jnp.arange(rows_dev, dtype=jnp.int32)
    rows = jnp.concatenate([found % all_rows, dest * rows_dev + joined, own_rows])
    lookup = (me ^ (rows // rows_dev)) * rows_dev + rows % rows_dev
    counts = jnp.concatenate(
        [
            found // all_rows,
            jnp.where(done == 1, page_len, 0).astype(jnp.int32),
            jnp.zeros((rows_dev,), jnp.int32),
        ]
    )
    fresh = jnp.pad(new_kv, ((0, 0), (0, page_len - steps), (0, 0), (0, 0)))
    fresh = fresh.reshape(rows_dev * page_len * 2, width_kv)

    parts, mls = pl.pallas_call(
        functools.partial(attend_kernel, rows_dev, n, len(blocks)),
        out_shape=(
            jax.ShapeDtypeStruct((n, block, HS), jnp.bfloat16),
            jax.ShapeDtypeStruct((n, 8, block), jnp.float32),
        ),
        in_specs=[smem()] * 3 + [vmem()] * (4 + len(blocks)),
        out_specs=(vmem(), vmem()),
        scratch_shapes=[pltpu.VMEM((n * block, 2 * HS), jnp.bfloat16)]
        + [pltpu.VMEM((n * block, HS), jnp.float32)] * 3,
        compiler_params=pltpu.CompilerParams(vmem_limit_bytes=VMEM_LIMIT),
    )(
        rows, counts, lookup, pool, prompt_kv[0], prompt_kv[1], fresh, *blocks,
    )

    merged = pl.pallas_call(
        functools.partial(merge_kernel, n),
        out_shape=jax.ShapeDtypeStruct((block, HS), jnp.bfloat16),
        in_specs=[vmem(), vmem()],
        out_specs=vmem(),
        scratch_shapes=[
            pltpu.VMEM((n, block, HS), jnp.bfloat16),
            pltpu.VMEM((n, 8, block), jnp.float32),
            pltpu.VMEM((HS, block), jnp.float32),
            pltpu.SemaphoreType.DMA((2, n)),
            pltpu.SemaphoreType.DMA((2, n)),
        ],
        compiler_params=pltpu.CompilerParams(
            collective_id=1, has_side_effects=True, vmem_limit_bytes=VMEM_LIMIT
        ),
    )(parts, mls)
    heads = merged.reshape(rows_dev, kv_heads, steps, group, HS).transpose(0, 2, 1, 3, 4)
    return heads.reshape(rows_dev, steps, width_q)


def solution(mesh):
    return jax.shard_map(
        body,
        mesh=mesh,
        in_specs=(
            P(("groups", "section"), None),
            P(),
            P(None, None, "tensor"),
            P(("groups", "section"), None, None, "tensor"),
            P(("groups", "section"), None, "tensor"),
            P(("groups", "section"), None, None, "tensor"),
            P("groups", None),
            P("groups"),
            P("groups"),
            P("groups", None),
            P("groups"),
        ),
        out_specs=P(("groups", "section"), None, "tensor"),
        check_vma=False,
    )
```

```python
import functools
import math

import jax
import jax.numpy as jnp
from jax import lax
from jax.experimental import pallas as pl
from jax.experimental.pallas import tpu as pltpu
from jax.sharding import PartitionSpec as P

HS = 128
MESH = pl.DeviceIdType.MESH
masked_value = -1e30
norm_epsilon = 1e-05
VMEM_LIMIT = 48 * 1024 * 1024
UNROLL = 8
ROW_BITS = 16
ROW_MASK = (1 << ROW_BITS) - 1


def vmem():
    return pl.BlockSpec(memory_space=pltpu.VMEM)


def smem():
    return pl.BlockSpec(memory_space=pltpu.SMEM)


def greet(n, me):
    barrier = pltpu.get_barrier_semaphore()
    for k in range(1, n):
        pl.semaphore_signal(
            barrier, inc=1, device_id={"section": lax.rem(me + k, n)}, device_id_type=MESH
        )
    pl.semaphore_wait(barrier, n - 1)


def attend_kernel(
    rows_dev, n, pieces, found_ref, dest_ref, joined_ref, done_ref, pool, prompt_k, prompt_v, fresh,
    *others
):
    blocks = others[:pieces]
    out_ref, ml_ref, q_ref, acc, tops, totals = others[pieces:]
    span = q_ref.shape[0] // (n * rows_dev)
    half = span // 2
    start = 0
    for piece in blocks:
        size = piece.shape[0]
        q = piece[...]
        of_low = lax.rem(lax.broadcasted_iota(jnp.int32, q.shape, 0), span) < half
        zero = jnp.zeros_like(q)
        q_ref[start : start + size, :HS] = jnp.where(of_low, q, zero)
        q_ref[start : start + size, HS:] = jnp.where(of_low, zero, q)
        start += size
    page_len = 64
    wide = 2 * page_len
    pool_pages = pool.shape[0] // wide
    prompt_pages = prompt_k.shape[0] // page_len
    scale = 1.0 / math.sqrt(HS)
    acc[...] = jnp.zeros_like(acc)
    totals[...] = jnp.zeros_like(totals)
    tops[...] = jnp.full_like(tops, masked_value)
    lane = lax.broadcasted_iota(jnp.int32, (span, wide), 1)
    line = lax.broadcasted_iota(jnp.int32, (span, wide), 0)
    step = lax.rem(line, half) // 8
    twice = jnp.where(lax.rem(lane, 2) == 0, lane // 2, page_len)
    contract_last = (((1,), (1,)), ((), ()))

    me = lax.axis_index("section")
    steps = fresh.shape[0] // (2 * rows_dev)
    fresh_kv = jnp.concatenate(
        [fresh[...], jnp.zeros((wide - fresh.shape[0], 2 * HS), fresh.dtype)], axis=0
    )

    def load_pair(ref, at):
        return ref[pl.ds(pl.multiple_of(at * wide, wide), wide), :]

    def load_split(refs, at):
        here = pl.ds(pl.multiple_of(at * page_len, page_len), page_len)
        return jnp.concatenate([refs[0][here, :], refs[1][here, :]], axis=0)

    def page_part(place, count, pages, at, kind):
        q = q_ref[pl.ds(pl.multiple_of(place * span, span), span), :]
        if kind == "split":
            kv = load_split(pages, at)
        elif kind == "fresh":
            kv = fresh_kv
        else:
            kv = load_pair(pages, at)
        scores = lax.dot_general(
            q, kv, contract_last, preferred_element_type=jnp.float32
        ) * scale
        if kind == "split":
            usable = lane < count
        elif kind == "fresh":
            since = twice - at * steps
            usable = (since >= 0) & (since <= step)
        else:
            usable = twice < count
        scores = jnp.where(usable, scores, masked_value)
        top = jnp.max(scores, axis=1, keepdims=True)
        weights = jnp.where(usable, jnp.exp(scores - top), 0.0)
        total = jnp.sum(weights, axis=1, keepdims=True)
        weights = pltpu.roll(weights, page_len if kind == "split" else 1, 1)
        main = weights.astype(jnp.bfloat16)
        rest = (weights - main.astype(jnp.float32)).astype(jnp.bfloat16)
        both_low = jnp.concatenate([main[:half], rest[:half]], axis=0)
        both_high = jnp.concatenate([main[half:], rest[half:]], axis=0)
        sum_low = jnp.dot(both_low, kv[:, :HS], preferred_element_type=jnp.float32)
        sum_high = jnp.dot(both_high, kv[:, HS:], preferred_element_type=jnp.float32)
        summed = jnp.concatenate(
            [sum_low[:half] + sum_low[half:], sum_high[:half] + sum_high[half:]], axis=0
        )
        return top, total, summed

    def update(row, part):
        top, total, summed = part
        place = pl.ds(pl.multiple_of(row * span, span), span)
        old = tops[place, :]
        new = jnp.maximum(old, top)
        keep = jnp.exp(old - new)
        add = jnp.exp(top - new)
        tops[place, :] = new
        totals[place, :] = totals[place, :] * keep + total * add
        acc[place, :] = acc[place, :] * keep + summed * add

    def pool_place(at):
        packed = found_ref[at]
        return jnp.bitwise_and(packed, ROW_MASK), jnp.right_shift(packed, ROW_BITS)

    def prompt_place(at):
        page = me * prompt_pages + at
        count = jnp.where(done_ref[page] == 1, page_len, 0)
        return dest_ref[page] * rows_dev + joined_ref[page], count

    def fresh_place(at):
        return me * rows_dev + at, steps

    def run(where, count, pages, kind):
        many = math.gcd(count, UNROLL)

        def some(i, _):
            parts = []
            for u in range(many):
                at = i * many + u
                row, live = where(at)
                owner = row // rows_dev
                place = jnp.bitwise_xor(me, owner) * rows_dev + (row - owner * rows_dev)
                parts.append((row, page_part(place, live, pages, at, kind)))
            for row, part in parts:
                update(row, part)
            return 0

        lax.fori_loop(0, count // many, some, 0)

    run(pool_place, pool_pages, pool, "pair")
    run(prompt_place, prompt_pages, (prompt_k, prompt_v), "split")
    run(fresh_place, rows_dev, None, "fresh")

    block = rows_dev * span
    lane = lax.broadcasted_iota(jnp.int32, (block, HS), 1)
    for d in range(n):
        here = pl.ds(d * block, block)
        out_ref[d] = acc[here, :].astype(jnp.bfloat16)
        mixed = jnp.where(lane == 0, tops[here, :], totals[here, :])
        ml_ref[d] = mixed.T[:8, :]


def merge_kernel(n, part_ref, ml_ref, out_ref, parts, mls, coef, send_sem, recv_sem):
    me = lax.axis_index("section")
    greet(n, me)
    copies = []
    for k in range(1, n):
        to = lax.rem(me + k, n)
        for which, (src, dst) in enumerate(((part_ref, parts), (ml_ref, mls))):
            copy = pltpu.make_async_remote_copy(
                src_ref=src.at[to],
                dst_ref=dst.at[me],
                send_sem=send_sem.at[which, k],
                recv_sem=recv_sem.at[which, k],
                device_id={"section": to},
                device_id_type=MESH,
            )
            copy.start()
            copies.append(copy)
    parts[me] = part_ref[me]
    mls[me] = ml_ref[me]
    for copy in copies:
        copy.wait()
    top = mls[0, 0:1, :]
    for i in range(1, n):
        top = jnp.maximum(top, mls[i, 0:1, :])
    total = jnp.zeros_like(top)
    for i in range(n):
        total = total + jnp.exp(mls[i, 0:1, :] - top) * mls[i, 1:2, :]
    coef[...] = jnp.zeros_like(coef)
    for i in range(n):
        coef[i : i + 1, :] = jnp.exp(mls[i, 0:1, :] - top) / total
    columns = coef[...].T
    result = jnp.zeros(out_ref.shape, jnp.float32)
    for i in range(n):
        result = result + parts[i].astype(jnp.float32) * columns[:, i : i + 1]
    out_ref[...] = result.astype(jnp.bfloat16)


def row_spread(prompts):
    states = prompts.astype(jnp.float32)
    return lax.rsqrt(jnp.mean(states * states, axis=-1, keepdims=True) + norm_epsilon)


def body(
    prompt_states,
    norm_gain,
    w_kv,
    pool_cache,
    queries,
    new_kv,
    ship_dest,
    page_row,
    finished,
    page_table,
    row_length,
):
    n = lax.axis_size("section")
    me = lax.axis_index("section")
    rows_dev, steps, width_q = queries.shape
    pool_pages, page_len, _, width_kv = pool_cache.shape
    kv_heads = width_kv // HS
    group = width_q // width_kv
    prompt_pages = prompt_states.shape[0] // page_len
    all_rows, max_pages = page_table.shape
    span = kv_heads * steps * group
    block = rows_dev * span

    own_q = queries.reshape(rows_dev, steps, kv_heads, group, HS).transpose(0, 2, 1, 3, 4)
    own_q = own_q.reshape(block, HS)
    blocks = [own_q]
    pool = pool_cache.reshape(pool_pages * page_len * 2, width_kv)
    prompts = prompt_states
    spread = None
    size = 1
    while size < n:
        whole = blocks[0] if size == 1 else jnp.concatenate(blocks, axis=0)
        other = lax.ppermute(whole, "section", [(i, i ^ size) for i in range(n)])
        if 2 * size == n:
            pass
        elif size == 1:
            other, pool, prompts = lax.optimization_barrier((other, pool, prompts))
        elif 4 * size == n:
            spread = row_spread(prompts)
            other, spread = lax.optimization_barrier((other, spread))
        blocks.append(other)
        size *= 2
    if spread is None:
        spread = row_spread(prompts)
    states = prompts.astype(jnp.float32)
    normed = (states * spread * norm_gain.astype(jnp.float32)).astype(jnp.bfloat16)
    prompt_kv = jnp.einsum("td,dkc->ktc", normed, w_kv, preferred_element_type=jnp.float32).astype(
        jnp.bfloat16
    )

    page_ids = me * pool_pages + jnp.arange(pool_pages, dtype=jnp.int32)
    page_hits = page_table[:, :, None] == page_ids[None, None, :]
    token_fill = jnp.clip(
        row_length[:, None] - jnp.arange(max_pages, dtype=jnp.int32)[None, :] * page_len,
        0,
        page_len,
    )
    row_ids = jnp.arange(all_rows, dtype=jnp.int32)
    packed = token_fill * (1 << ROW_BITS) + row_ids[:, None]
    found = jnp.sum(jnp.where(page_hits, packed[:, :, None], 0), axis=(0, 1))
    fresh = new_kv.reshape(rows_dev * steps * 2, width_kv)

    parts, mls = pl.pallas_call(
        functools.partial(attend_kernel, rows_dev, n, len(blocks)),
        out_shape=(
            jax.ShapeDtypeStruct((n, block, HS), jnp.bfloat16),
            jax.ShapeDtypeStruct((n, 8, block), jnp.float32),
        ),
        in_specs=[smem()] * 4 + [vmem()] * (4 + len(blocks)),
        out_specs=(vmem(), vmem()),
        scratch_shapes=[pltpu.VMEM((n * block, 2 * HS), jnp.bfloat16)]
        + [pltpu.VMEM((n * block, HS), jnp.float32)] * 3,
        compiler_params=pltpu.CompilerParams(vmem_limit_bytes=VMEM_LIMIT),
    )(
        found, ship_dest.reshape(-1), page_row, finished, pool, prompt_kv[0], prompt_kv[1], fresh, *blocks,
    )

    merged = pl.pallas_call(
        functools.partial(merge_kernel, n),
        out_shape=jax.ShapeDtypeStruct((block, HS), jnp.bfloat16),
        in_specs=[vmem(), vmem()],
        out_specs=vmem(),
        scratch_shapes=[
            pltpu.VMEM((n, block, HS), jnp.bfloat16),
            pltpu.VMEM((n, 8, block), jnp.float32),
            pltpu.VMEM((HS, block), jnp.float32),
            pltpu.SemaphoreType.DMA((2, n)),
            pltpu.SemaphoreType.DMA((2, n)),
        ],
        compiler_params=pltpu.CompilerParams(
            collective_id=1, has_side_effects=True, vmem_limit_bytes=VMEM_LIMIT
        ),
    )(parts, mls)
    heads = merged.reshape(rows_dev, kv_heads, steps, group, HS).transpose(0, 2, 1, 3, 4)
    return heads.reshape(rows_dev, steps, width_q)


def solution(mesh):
    return jax.shard_map(
        body,
        mesh=mesh,
        in_specs=(
            P(("groups", "section"), None),
            P(),
            P(None, None, "tensor"),
            P(("groups", "section"), None, None, "tensor"),
            P(("groups", "section"), None, "tensor"),
            P(("groups", "section"), None, None, "tensor"),
            P("groups", None),
            P("groups"),
            P("groups"),
            P("groups", None),
            P("groups"),
        ),
        out_specs=P(("groups", "section"), None, "tensor"),
        check_vma=False,
    )
```

```python
import functools
import math

import jax
import jax.numpy as jnp
from jax import lax
from jax.experimental import pallas as pl
from jax.experimental.pallas import tpu as pltpu
from jax.sharding import PartitionSpec as P

HS = 128
MESH = pl.DeviceIdType.MESH
masked_value = -1e30
norm_epsilon = 1e-05
VMEM_LIMIT = 48 * 1024 * 1024
UNROLL = 8
ROW_BITS = 16
ROW_MASK = (1 << ROW_BITS) - 1


def vmem():
    return pl.BlockSpec(memory_space=pltpu.VMEM)


def smem():
    return pl.BlockSpec(memory_space=pltpu.SMEM)


def greet(n, me):
    barrier = pltpu.get_barrier_semaphore()
    for k in range(1, n):
        pl.semaphore_signal(
            barrier, inc=1, device_id={"section": lax.rem(me + k, n)}, device_id_type=MESH
        )
    pl.semaphore_wait(barrier, n - 1)


def attend_kernel(
    rows_dev, n, pieces, found_ref, dest_ref, joined_ref, done_ref, pool, prompt_k, prompt_v, fresh,
    *others
):
    blocks = others[:pieces]
    out_ref, ml_ref, q_ref, acc, tops, totals = others[pieces:]
    span = q_ref.shape[0] // (n * rows_dev)
    half = span // 2
    start = 0
    for piece in blocks:
        size = piece.shape[0]
        q = piece[...]
        of_low = lax.rem(lax.broadcasted_iota(jnp.int32, q.shape, 0), span) < half
        zero = jnp.zeros_like(q)
        q_ref[start : start + size, :HS] = jnp.where(of_low, q, zero)
        q_ref[start : start + size, HS:] = jnp.where(of_low, zero, q)
        start += size
    page_len = 64
    wide = 2 * page_len
    pool_pages = pool.shape[0]
    prompt_pages = prompt_k.shape[0] // page_len
    scale = 1.0 / math.sqrt(HS)
    acc[...] = jnp.zeros_like(acc)
    totals[...] = jnp.zeros_like(totals)
    tops[...] = jnp.full_like(tops, masked_value)
    lane = lax.broadcasted_iota(jnp.int32, (span, wide), 1)
    line = lax.broadcasted_iota(jnp.int32, (span, wide), 0)
    step = lax.rem(line, half) // 8
    twice = jnp.where(lax.rem(lane, 2) == 0, lane // 2, page_len)
    contract_last = (((1,), (1,)), ((), ()))

    me = lax.axis_index("section")
    steps = fresh.shape[0] // (2 * rows_dev)
    fresh_kv = jnp.concatenate(
        [fresh[...], jnp.zeros((wide - fresh.shape[0], 2 * HS), fresh.dtype)], axis=0
    )

    def load_pair(ref, at):
        return ref[at].reshape(wide, 2 * HS)

    def load_split(refs, at):
        here = pl.ds(pl.multiple_of(at * page_len, page_len), page_len)
        return jnp.concatenate([refs[0][here, :], refs[1][here, :]], axis=0)

    def page_part(place, count, pages, at, kind):
        q = q_ref[pl.ds(pl.multiple_of(place * span, span), span), :]
        if kind == "split":
            kv = load_split(pages, at)
        elif kind == "fresh":
            kv = fresh_kv
        else:
            kv = load_pair(pages, at)
        scores = lax.dot_general(
            q, kv, contract_last, preferred_element_type=jnp.float32
        ) * scale
        if kind == "split":
            usable = lane < count
        elif kind == "fresh":
            since = twice - at * steps
            usable = (since >= 0) & (since <= step)
        else:
            usable = twice < count
        scores = jnp.where(usable, scores, masked_value)
        top = jnp.max(scores, axis=1, keepdims=True)
        weights = jnp.where(usable, jnp.exp(scores - top), 0.0)
        total = jnp.sum(weights, axis=1, keepdims=True)
        weights = pltpu.roll(weights, page_len if kind == "split" else 1, 1)
        main = weights.astype(jnp.bfloat16)
        rest = (weights - main.astype(jnp.float32)).astype(jnp.bfloat16)
        both_low = jnp.concatenate([main[:half], rest[:half]], axis=0)
        both_high = jnp.concatenate([main[half:], rest[half:]], axis=0)
        sum_low = jnp.dot(both_low, kv[:, :HS], preferred_element_type=jnp.float32)
        sum_high = jnp.dot(both_high, kv[:, HS:], preferred_element_type=jnp.float32)
        summed = jnp.concatenate(
            [sum_low[:half] + sum_low[half:], sum_high[:half] + sum_high[half:]], axis=0
        )
        return top, total, summed

    def update(row, part):
        top, total, summed = part
        place = pl.ds(pl.multiple_of(row * span, span), span)
        old = tops[place, :]
        new = jnp.maximum(old, top)
        keep = jnp.exp(old - new)
        add = jnp.exp(top - new)
        tops[place, :] = new
        totals[place, :] = totals[place, :] * keep + total * add
        acc[place, :] = acc[place, :] * keep + summed * add

    def pool_place(at):
        packed = found_ref[at]
        return jnp.bitwise_and(packed, ROW_MASK), jnp.right_shift(packed, ROW_BITS)

    def prompt_place(at):
        page = me * prompt_pages + at
        count = jnp.where(done_ref[page] == 1, page_len, 0)
        return dest_ref[page] * rows_dev + joined_ref[page], count

    def fresh_place(at):
        return me * rows_dev + at, steps

    def run(where, count, pages, kind):
        many = math.gcd(count, UNROLL)

        def some(i, _):
            parts = []
            for u in range(many):
                at = i * many + u
                row, live = where(at)
                owner = row // rows_dev
                place = jnp.bitwise_xor(me, owner) * rows_dev + (row - owner * rows_dev)
                parts.append((row, page_part(place, live, pages, at, kind)))
            for row, part in parts:
                update(row, part)
            return 0

        lax.fori_loop(0, count // many, some, 0)

    run(pool_place, pool_pages, pool, "pair")
    run(prompt_place, prompt_pages, (prompt_k, prompt_v), "split")
    run(fresh_place, rows_dev, None, "fresh")

    block = rows_dev * span
    lane = lax.broadcasted_iota(jnp.int32, (block, HS), 1)
    for d in range(n):
        here = pl.ds(d * block, block)
        out_ref[d] = acc[here, :].astype(jnp.bfloat16)
        mixed = jnp.where(lane == 0, tops[here, :], totals[here, :])
        ml_ref[d] = mixed.T[:8, :]


def merge_kernel(n, part_ref, ml_ref, out_ref, parts, mls, coef, send_sem, recv_sem):
    me = lax.axis_index("section")
    greet(n, me)
    copies = []
    for k in range(1, n):
        to = lax.rem(me + k, n)
        for which, (src, dst) in enumerate(((part_ref, parts), (ml_ref, mls))):
            copy = pltpu.make_async_remote_copy(
                src_ref=src.at[to],
                dst_ref=dst.at[me],
                send_sem=send_sem.at[which, k],
                recv_sem=recv_sem.at[which, k],
                device_id={"section": to},
                device_id_type=MESH,
            )
            copy.start()
            copies.append(copy)
    parts[me] = part_ref[me]
    mls[me] = ml_ref[me]
    for copy in copies:
        copy.wait()
    top = mls[0, 0:1, :]
    for i in range(1, n):
        top = jnp.maximum(top, mls[i, 0:1, :])
    total = jnp.zeros_like(top)
    for i in range(n):
        total = total + jnp.exp(mls[i, 0:1, :] - top) * mls[i, 1:2, :]
    coef[...] = jnp.zeros_like(coef)
    for i in range(n):
        coef[i : i + 1, :] = jnp.exp(mls[i, 0:1, :] - top) / total
    columns = coef[...].T
    result = jnp.zeros(out_ref.shape, jnp.float32)
    for i in range(n):
        result = result + parts[i].astype(jnp.float32) * columns[:, i : i + 1]
    out_ref[...] = result.astype(jnp.bfloat16)


def row_spread(prompts):
    states = prompts.astype(jnp.float32)
    return lax.rsqrt(jnp.mean(states * states, axis=-1, keepdims=True) + norm_epsilon)


def body(
    prompt_states,
    norm_gain,
    w_kv,
    pool_cache,
    queries,
    new_kv,
    ship_dest,
    page_row,
    finished,
    page_table,
    row_length,
):
    n = lax.axis_size("section")
    me = lax.axis_index("section")
    rows_dev, steps, width_q = queries.shape
    pool_pages, page_len, _, width_kv = pool_cache.shape
    kv_heads = width_kv // HS
    group = width_q // width_kv
    prompt_pages = prompt_states.shape[0] // page_len
    all_rows, max_pages = page_table.shape
    span = kv_heads * steps * group
    block = rows_dev * span

    own_q = queries.reshape(rows_dev, steps, kv_heads, group, HS).transpose(0, 2, 1, 3, 4)
    own_q = own_q.reshape(block, HS)
    blocks = [own_q]
    pool = pool_cache
    prompts = prompt_states
    spread = None
    size = 1
    while size < n:
        whole = blocks[0] if size == 1 else jnp.concatenate(blocks, axis=0)
        other = lax.ppermute(whole, "section", [(i, i ^ size) for i in range(n)])
        if 2 * size == n:
            pass
        elif size == 1:
            other, pool, prompts = lax.optimization_barrier((other, pool, prompts))
        elif 4 * size == n:
            spread = row_spread(prompts)
            other, spread = lax.optimization_barrier((other, spread))
        blocks.append(other)
        size *= 2
    if spread is None:
        spread = row_spread(prompts)
    states = prompts.astype(jnp.float32)
    normed = (states * spread * norm_gain.astype(jnp.float32)).astype(jnp.bfloat16)
    prompt_kv = jnp.einsum("td,dkc->ktc", normed, w_kv, preferred_element_type=jnp.float32).astype(
        jnp.bfloat16
    )

    page_ids = me * pool_pages + jnp.arange(pool_pages, dtype=jnp.int32)
    page_hits = page_table[:, :, None] == page_ids[None, None, :]
    token_fill = jnp.clip(
        row_length[:, None] - jnp.arange(max_pages, dtype=jnp.int32)[None, :] * page_len,
        0,
        page_len,
    )
    row_ids = jnp.arange(all_rows, dtype=jnp.int32)
    packed = token_fill * (1 << ROW_BITS) + row_ids[:, None]
    found = jnp.sum(jnp.where(page_hits, packed[:, :, None], 0), axis=(0, 1))
    fresh = new_kv.reshape(rows_dev * steps * 2, width_kv)

    parts, mls = pl.pallas_call(
        functools.partial(attend_kernel, rows_dev, n, len(blocks)),
        out_shape=(
            jax.ShapeDtypeStruct((n, block, HS), jnp.bfloat16),
            jax.ShapeDtypeStruct((n, 8, block), jnp.float32),
        ),
        in_specs=[smem()] * 4 + [vmem()] * (4 + len(blocks)),
        out_specs=(vmem(), vmem()),
        scratch_shapes=[pltpu.VMEM((n * block, 2 * HS), jnp.bfloat16)]
        + [pltpu.VMEM((n * block, HS), jnp.float32)] * 3,
        compiler_params=pltpu.CompilerParams(vmem_limit_bytes=VMEM_LIMIT),
    )(
        found, ship_dest.reshape(-1), page_row, finished, pool, prompt_kv[0], prompt_kv[1], fresh, *blocks,
    )

    merged = pl.pallas_call(
        functools.partial(merge_kernel, n),
        out_shape=jax.ShapeDtypeStruct((block, HS), jnp.bfloat16),
        in_specs=[vmem(), vmem()],
        out_specs=vmem(),
        scratch_shapes=[
            pltpu.VMEM((n, block, HS), jnp.bfloat16),
            pltpu.VMEM((n, 8, block), jnp.float32),
            pltpu.VMEM((HS, block), jnp.float32),
            pltpu.SemaphoreType.DMA((2, n)),
            pltpu.SemaphoreType.DMA((2, n)),
        ],
        compiler_params=pltpu.CompilerParams(
            collective_id=1, has_side_effects=True, vmem_limit_bytes=VMEM_LIMIT
        ),
    )(parts, mls)
    heads = merged.reshape(rows_dev, kv_heads, steps, group, HS).transpose(0, 2, 1, 3, 4)
    return heads.reshape(rows_dev, steps, width_q)


def solution(mesh):
    return jax.shard_map(
        body,
        mesh=mesh,
        in_specs=(
            P(("groups", "section"), None),
            P(),
            P(None, None, "tensor"),
            P(("groups", "section"), None, None, "tensor"),
            P(("groups", "section"), None, "tensor"),
            P(("groups", "section"), None, None, "tensor"),
            P("groups", None),
            P("groups"),
            P("groups"),
            P("groups", None),
            P("groups"),
        ),
        out_specs=P(("groups", "section"), None, "tensor"),
        check_vma=False,
    )
```
